256 devices in a mesh: dp: 64 (over z, y, core), tensor: 4 (over x).
Axes of the slice: x: 4, y: 4, z: 8, core: 2. Of those that a mesh axis runs over, the one named last changes fastest.
Arguments:
- queries: bfloat16 [8192, 4096], P('dp', 'tensor'), may hold values from -6 to 6
- keys: bfloat16 [160, 1792, 512], P(None, ('dp', 'tensor')), may hold values from -4.375 to 4.375
- values: bfloat16 [160, 1792, 512], P(None, ('dp', 'tensor')), may hold values from -6 to 6
- d_out: bfloat16 [8192, 4096], P('dp', 'tensor'), may hold values from -6 to 6
- tile_sample: int32 [160], replicated, may hold values from 0 to 127, as said below
- row_sample: int32 [64, 128], P('dp'), may hold values from 0 to 1, never falling along the last dimension, each value on 1 to 96 neighbouring positions
Outputs:
- attn_out: bfloat16 [8192, 4096], P('dp', 'tensor')
- d_query: bfloat16 [8192, 4096], P('dp', 'tensor')
- d_key: bfloat16 [160, 1792, 512], P(None, ('dp', 'tensor'))
- d_value: bfloat16 [160, 1792, 512], P(None, ('dp', 'tensor'))
The draws below stay inside these ranges and needn't reach their ends.
Inputs may be any that keep to these rules, and one draw needn't show every extreme that they name: `tile_sample`: every sample has one or two tiles; the samples of one text device have at most 3 tiles together, and some text device has exactly 3.
All inputs are finite; a program needn't handle non-finite values.
Results may differ from the reference program's by a relative error of at most 0.015.
Values may be sent and summed in bfloat16 or wider, within the bound.
No kernel may reach another device: no remote copies, remote signals or barrier semaphores. Data moves between devices by JAX's collectives and lax.ppermute only.
A program may use at most 192 MiB of HBM per device.

```python
import math
import jax
import jax.numpy as jnp
import numpy as np
from jax import lax

HD = 128
QH = 32
KVH = 4
PATCHES = 1601
TXT_DEV = 128
SMP_DEV = 2
MAXT_DEV = 3
SAMPLES = 128
TEXT = 8192
TILES = 160
TILE_PAD = 1792
N_DP = 64


def draw_queries(key, part):
    key = jax.random.fold_in(key, 3)
    result = 2.0 * jnp.clip(jax.random.normal(key, (TEXT, QH * HD), jnp.float32), -3.0, 3.0)
    return result.astype(jnp.bfloat16)


def draw_keys(key, part):
    key = jax.random.fold_in(key, 4)
    result = jnp.clip(jax.random.normal(key, (TILES, TILE_PAD, KVH * HD), jnp.float32), -4.0, 4.0)
    return result.astype(jnp.bfloat16)


def draw_tile_sample(key, part):
    key = jax.random.fold_in(key, 5)
    pick_key, side_key, order_key = jax.random.split(key, 3)
    device_count = SAMPLES // SMP_DEV
    candidate = jnp.arange(device_count, dtype=jnp.int32)
    candidate_sample = candidate * SMP_DEV + jax.random.randint(side_key, (device_count,), 0, SMP_DEV, dtype=jnp.int32)
    ranking = jax.random.permutation(pick_key, device_count).astype(jnp.int32)
    chosen = jnp.argsort(ranking, stable=True)[:device_count // 2]
    extra_tiles = candidate_sample[chosen]
    single_tiles = jnp.arange(SAMPLES, dtype=jnp.int32)
    all_tiles = jnp.concatenate([single_tiles, extra_tiles])
    shuffle = jax.random.permutation(order_key, TILES)
    return all_tiles[shuffle].astype(jnp.int32)


def block_levels(rng, extent, cuts, smallest, top_value):
    def one(position, parts):
        steps = jax.random.uniform(jax.random.fold_in(jax.random.fold_in(rng, 6), position), (parts,), jnp.float32, smallest / len(cuts), top_value / len(cuts))
        return jnp.repeat(jnp.exp(steps), extent[position] // parts).reshape((-1,) + (1,) * (len(extent) - position - 1))

    level = one(*cuts[0])
    for cut in cuts[1:]:
        level = level * one(*cut)
    return level


def profile(amount, total, reach, skew):
    portions = [(1 << 20) // math.isqrt(grade ** skew) + 1 for grade in range(2, amount + 1)]
    spare, given = total - reach - (amount - 1), [1] * (amount - 1)
    while spare > 0:
        free = [i for i in range(amount - 1) if given[i] < reach]
        whole, budget = sum([portions[i] for i in free]), spare
        for i in free:
            more = min(reach - given[i], max(1, budget * portions[i] // whole), spare)
            given[i] = given[i] + more
            spare = spare - more
    return np.array([reach] + given)


def uneven_parts(own_key, number_of, total, most, skew):
    if number_of == 2:
        one = jax.random.randint(own_key, (), max(1, total - most), min(most, total - 1) + 1)
        return jnp.stack([one, total - one])
    tallies = jnp.asarray(profile(number_of, total, most, skew), jnp.int32)
    twos = (number_of - 1) // 2
    donor, receiver = tallies[1:1 + 2 * twos:2], tallies[2:2 + 2 * twos:2]
    room = jnp.minimum(donor - 1, most - receiver)
    passed = jax.random.randint(jax.random.fold_in(own_key, 1), (twos,), 0, 1 << 20) % (room + 1)
    tallies = tallies.at[1:1 + 2 * twos:2].set(donor - passed).at[2:2 + 2 * twos:2].set(receiver + passed)
    return tallies[jax.random.permutation(jax.random.fold_in(own_key, 2), number_of)]


def normal_values(own_key, shape, spread, bound, pieces=(), held_as=jnp.bfloat16):
    entries = jax.random.normal(own_key, shape, jnp.float32) * spread
    if len(pieces) > 0:
        entries = block_levels(own_key, shape, pieces, -0.22, 0.18) * entries
    return jnp.clip(entries, min=-bound, max=bound).astype(held_as)


def setup_inputs(seed: int = 0) -> dict:
    splits = jax.random.split(jax.random.key(seed), 7)
    return {
        "queries": draw_queries(jax.random.fold_in(splits[6], 71), 0),
        "keys": draw_keys(jax.random.fold_in(splits[6], 71), 0),
        "values": normal_values(splits[2], (TILES, TILE_PAD, KVH * HD), 1.0, 6.0, ((1, 256),)),
        "d_out": normal_values(splits[3], (TEXT, QH * HD), 1.0, 6.0, ((0, 64), (1, 4))),
        "tile_sample": draw_tile_sample(jax.random.fold_in(splits[6], 71), 0),
        "row_sample": jax.vmap(lambda own: jnp.searchsorted(jnp.cumsum(uneven_parts(own, SMP_DEV, TXT_DEV, TXT_DEV * 3 // 4, 0)), jnp.arange(TXT_DEV), side="right"))(jax.random.split(splits[5], N_DP)).reshape((N_DP, TXT_DEV)).astype(jnp.int32),
    }


def slot_table(tile_sample, dp_count):
    owner_dev = tile_sample // SMP_DEV
    member = (owner_dev[None, :] == jnp.arange(dp_count, dtype=jnp.int32)[:, None]).astype(jnp.int32)
    ranking = jnp.cumsum(member, axis=1, dtype=jnp.int32) * member
    matches = (ranking[:, None, :] == jnp.arange(1, MAXT_DEV + 1, dtype=jnp.int32)[None, :, None]).astype(jnp.int32)
    tile_ids = jnp.arange(tile_sample.shape[0], dtype=jnp.int32)
    slot_tile = lax.optimization_barrier(jnp.sum(matches * tile_ids[None, None, :], axis=2, dtype=jnp.int32))
    slot_used = lax.optimization_barrier(jnp.sum(matches, axis=2, dtype=jnp.int32)) > 0
    slot_sample = lax.optimization_barrier(jnp.sum(matches * (tile_sample % SMP_DEV)[None, None, :], axis=2, dtype=jnp.int32))
    return (slot_tile, slot_used, slot_sample)

def attend(query_rows, image_key_rows, image_value_rows, grad_out, allowed):
    row_count = query_rows.shape[0]
    kv_heads = image_key_rows.shape[1] // HD
    group_size = QH // KVH
    scaling = 1.0 / math.sqrt(HD)
    highest = lax.Precision.HIGHEST
    query_piece = query_rows.astype(jnp.float32).reshape(row_count, kv_heads, group_size, HD)
    key_split = image_key_rows.astype(jnp.float32).reshape(-1, kv_heads, HD)
    value_split = image_value_rows.astype(jnp.float32).reshape(-1, kv_heads, HD)
    gradient_piece = grad_out.astype(jnp.float32).reshape(row_count, kv_heads, group_size, HD)
    logit_scores = jnp.einsum('rkgd,tkd->kgrt', query_piece, key_split, precision=highest)
    logit_scores = jnp.where(allowed[None, None], logit_scores * scaling, -1e+30)
    row_max = lax.optimization_barrier(jnp.max(logit_scores, axis=-1, keepdims=True))
    raised = jnp.exp(logit_scores - row_max)
    attention = raised / lax.optimization_barrier(jnp.sum(raised, axis=-1, keepdims=True))
    quantized_weights = lax.optimization_barrier(attention.astype(jnp.bfloat16)).astype(jnp.float32)
    output = jnp.einsum('kgrt,tkd->rkgd', quantized_weights, value_split, precision=highest)
    output = output.astype(jnp.bfloat16).reshape(row_count, -1)
    grad_weights = jnp.einsum('rkgd,tkd->kgrt', gradient_piece, value_split, precision=highest)
    row_delta = lax.optimization_barrier(jnp.sum(attention * grad_weights, axis=-1, keepdims=True))
    score_gradient = (attention * (grad_weights - row_delta) * scaling).astype(jnp.bfloat16)
    score_gradient = lax.optimization_barrier(score_gradient).astype(jnp.float32)
    grad_query = jnp.einsum('kgrt,tkd->rkgd', score_gradient, key_split, precision=highest)
    grad_query = grad_query.astype(jnp.bfloat16).reshape(row_count, -1)
    grad_key = jnp.einsum('kgrt,rkgd->tkd', score_gradient, query_piece, precision=highest)
    grad_key = grad_key.astype(jnp.bfloat16).reshape(image_key_rows.shape[0], -1)
    grad_value = jnp.einsum('kgrt,rkgd->tkd', quantized_weights, gradient_piece, precision=highest)
    grad_value = grad_value.astype(jnp.bfloat16).reshape(image_key_rows.shape[0], -1)
    return (output, grad_query, grad_key, grad_value)

def reference(queries, keys, values, d_out, tile_sample, row_sample):
    slot_tile, slot_used, slot_sample = slot_table(tile_sample, N_DP)
    token_ok = jnp.tile(jnp.arange(TILE_PAD) < PATCHES, MAXT_DEV)

    def visit(device, carry):
        grad_keys, grad_values, outputs, grad_queries = carry
        device = jnp.asarray(device).astype(jnp.int32)
        row_start = (device * TXT_DEV).astype(jnp.int32)
        query_rows = lax.dynamic_slice_in_dim(queries, row_start, TXT_DEV, 0)
        grad_rows = lax.dynamic_slice_in_dim(d_out, row_start, TXT_DEV, 0)
        tiles_here = slot_tile[device]
        used_here = slot_used[device]
        sample_here = slot_sample[device]
        image_key_rows = keys[tiles_here].reshape(MAXT_DEV * TILE_PAD, KVH * HD)
        image_value_rows = values[tiles_here].reshape(MAXT_DEV * TILE_PAD, KVH * HD)
        slot_ok = jnp.repeat(used_here, TILE_PAD) & token_ok
        same_sample = row_sample[device][:, None] == jnp.repeat(sample_here, TILE_PAD)[None, :]
        allowed = same_sample & slot_ok[None, :]
        output, grad_query, grad_key, grad_value = attend(query_rows, image_key_rows, image_value_rows, grad_rows, allowed)
        targets = jnp.where(used_here, tiles_here, TILES).astype(jnp.int32)
        grad_keys = grad_keys.at[targets].set(grad_key.reshape(MAXT_DEV, TILE_PAD, KVH * HD), mode='drop')
        grad_values = grad_values.at[targets].set(grad_value.reshape(MAXT_DEV, TILE_PAD, KVH * HD), mode='drop')
        outputs = lax.dynamic_update_slice_in_dim(outputs, output, row_start, 0)
        grad_queries = lax.dynamic_update_slice_in_dim(grad_queries, grad_query, row_start, 0)
        return (grad_keys, grad_values, outputs, grad_queries)
    initial = (jnp.zeros(keys.shape, jnp.bfloat16), jnp.zeros(values.shape, jnp.bfloat16), jnp.zeros(queries.shape, jnp.bfloat16), jnp.zeros(queries.shape, jnp.bfloat16))
    grad_keys, grad_values, outputs, grad_queries = lax.fori_loop(0, N_DP, visit, initial)
    return (outputs, grad_queries, grad_keys, grad_values)
```

```python
import functools
import math

import jax
import jax.numpy as jnp
from jax import lax
from jax.experimental import pallas as pl
from jax.experimental.pallas import tpu as pltpu
from jax.sharding import Mesh
from jax.sharding import PartitionSpec as P

HD = 128
QH = 32
KVH = 4
PATCHES = 1601
SMP_DEV = 2
MAXT = 3
NZ = 8
NC = 8
ROWS = 128
HEADS = QH // KVH
RB = 4
RBR = ROWS // RB
BL = HEADS * RBR
LANES = HEADS * ROWS
SLOTS = NZ * MAXT
TOKS = 256
WIDE = (RB - 1) * BL
HALF = NZ // 2
NQ = ROWS + 16
NEG = -1e30
SCALE = 1.0 / math.sqrt(HD)
SCALE2 = SCALE / math.log(2.0)
BF = jnp.bfloat16
F32 = jnp.float32
MIB = 1024 * 1024


def dot(a, b, ca, cb):
    return lax.dot_general(a, b, (((ca,), (cb,)), ((), ())), preferred_element_type=F32)


def select_kernel(spot_ref, k_ref, v_ref, out_ref, rows_ref):
    spots = spot_ref.shape[0]
    tiles = k_ref.shape[0] // 7
    width = k_ref.shape[1]
    col = lax.broadcasted_iota(jnp.int32, (spots, tiles), 1)
    pick = jnp.where(col == spot_ref[...], 1.0, 0.0).astype(BF)
    for j, ref in enumerate((k_ref, v_ref)):
        for n in range(7):
            rows = dot(pick, ref[n * tiles : (n + 1) * tiles], 1, 0)
            for x in range(width // HD):
                rows_ref[j, x, pl.ds(n, spots, stride=8), :] = rows[:, x * HD : (x + 1) * HD]
        for x in range(width // HD):
            rows_ref[j, x, pl.ds(7, spots, stride=8), :] = jnp.zeros((spots, HD), F32)
            for c in range(NC):
                out_ref[c, x, j] = rows_ref[j, x, c * SLOTS * 8 : (c + 1) * SLOTS * 8].astype(BF)


def return_kernel(spot_ref, recv_ref, dk_ref, dv_ref, rows_ref):
    spots = NC * SLOTS
    tiles = spot_ref.shape[0]
    col = lax.broadcasted_iota(jnp.int32, (tiles, spots), 1)
    pick = jnp.where(col == spot_ref[...], 1.0, 0.0).astype(BF)
    for j in range(2):
        rows_ref[j] = recv_ref[:, 0, j].astype(F32).reshape(spots * 8, HD)
    for n in range(7):
        both = jnp.concatenate(
            [rows_ref[j, pl.ds(n, spots, stride=8), :].astype(BF) for j in range(2)], axis=1
        )
        rows = dot(pick, both, 1, 0).astype(BF)
        dk_ref[n * tiles : (n + 1) * tiles] = rows[:, :HD]
        dv_ref[n * tiles : (n + 1) * tiles] = rows[:, HD:]


def pack_kernel(row_ref, q_ref, do_ref, out_ref):
    first = jnp.sum(jnp.where(row_ref[...] == 0, 1.0, 0.0)).astype(jnp.int32)
    lane = lax.broadcasted_iota(jnp.int32, (16, LANES), 1)
    row = (lane // BL) * RBR + lane % RBR
    out_ref[:ROWS] = q_ref[...]
    out_ref[ROWS:NQ] = jnp.where(row >= first, 1.0, 0.0).astype(BF)
    out_ref[NQ:] = do_ref[...]


def load_rows(pack_ref, q_ref, do_ref, qt_ref, dot_ref):
    for rb in range(RB):
        sl = slice(rb * BL, (rb + 1) * BL)
        for h in range(HEADS):
            lo = rb * BL + h * RBR
            cols = slice(h * HD, (h + 1) * HD)
            q_ref[lo : lo + RBR] = pack_ref[0, rb * RBR : (rb + 1) * RBR, cols]
            do_ref[lo : lo + RBR] = pack_ref[0, NQ + rb * RBR : NQ + (rb + 1) * RBR, cols]
        qt_ref[0:HD, sl] = q_ref[sl].T
        dot_ref[:, sl] = do_ref[sl].T
    sample = pack_ref[0, ROWS:NQ, :]
    row = lax.broadcasted_iota(jnp.int32, (16, LANES), 0)
    off = jnp.where(
        row == 0, 1.0,
        jnp.where(
            ((row == 1) & (sample.astype(F32) > 0.5)) | ((row == 2) & (sample.astype(F32) < 0.5)),
            NEG, 0.0,
        ),
    )
    qt_ref[HD : HD + 16] = off.astype(BF)


def set_up(z, qt_ref, side_ref):
    qt_ref[HD:] = jnp.zeros((HD, LANES), BF)
    i = lax.broadcasted_iota(jnp.int32, (TOKS, HD), 0)
    lane = lax.broadcasted_iota(jnp.int32, (TOKS, HD), 1)
    n = i % 8
    pos = z * 224 + (i // 8) * 7 + n
    empty = (n >= 7) | (pos >= PATCHES)
    for j in range(SMP_DEV + 1):
        none = empty if j < SMP_DEV else lane >= 0
        side_ref[j] = jnp.where(
            lane == 0, jnp.where(none, NEG, 0.0), jnp.where(lane == 1 + j, 1.0, 0.0)
        ).astype(BF)


def slot_tokens(kv_ref, j, s):
    return kv_ref[:, j, s].reshape(TOKS, HD)


def stats_kernel(half, slot_ref, pack_ref, kv_ref, stat_ref,
                 q_ref, do_ref, qt_ref, dot_ref, side_ref, m_ref, l_ref, d_ref):
    here = pl.program_id(0)
    text = half * HALF + here

    @pl.when(here == 0)
    def _():
        set_up(slot_ref[0], qt_ref, side_ref)

    load_rows(pack_ref, q_ref, do_ref, qt_ref, dot_ref)
    m_ref[...] = jnp.full(m_ref.shape, 2 * NEG, F32)
    l_ref[...] = jnp.zeros(l_ref.shape, F32)
    d_ref[...] = jnp.zeros(d_ref.shape, F32)

    def slot(s):
        mark = slot_ref[1 + text * MAXT + s]
        owner = jnp.maximum(mark, 0)
        side = side_ref[jnp.where(mark < 0, SMP_DEV, owner)]
        k = jnp.concatenate([slot_tokens(kv_ref, 0, s), side], axis=1)
        v = slot_tokens(kv_ref, 1, s)
        sl = pl.ds(pl.multiple_of(owner * BL, BL), WIDE)
        sc = dot(k, qt_ref[:, sl], 1, 0)
        g = dot(v, dot_ref[:, sl], 1, 0)
        top = jnp.max(sc, axis=0, keepdims=True)
        p = jnp.exp2((sc - top) * SCALE2)
        total = jnp.sum(p, axis=0, keepdims=True)
        delta = jnp.sum(p * g, axis=0, keepdims=True)
        old = m_ref[:, sl]
        new = jnp.maximum(old, top)
        a = jnp.exp2((old - new) * SCALE2)
        b = jnp.exp2((top - new) * SCALE2)
        m_ref[:, sl] = new
        l_ref[:, sl] = l_ref[:, sl] * a + total * b
        d_ref[:, sl] = d_ref[:, sl] * a + delta * b

    for s in range(MAXT):
        slot(s)
    lse = m_ref[...] + jnp.log2(l_ref[...]) * (1.0 / SCALE2)
    delta = d_ref[...] / l_ref[...]
    for i in range(NZ):
        stat_ref[i, pl.ds(here, 1), :] = lse
        stat_ref[i, pl.ds(HALF + here, 1), :] = delta


def grad_kernel(half, slot_ref, pack_ref, kv_ref, stat_ref, *refs):
    (rows_ref, dkv_ref, q_ref, do_ref, qt_ref, dot_ref, side_ref,
     lse_ref, delta_ref, dq_ref, out_ref) = refs[2 * half :]
    here = pl.program_id(0)
    text = half * HALF + here

    @pl.when(here == 0)
    def _():
        set_up(slot_ref[0], qt_ref, side_ref)

    load_rows(pack_ref, q_ref, do_ref, qt_ref, dot_ref)
    lses = [stat_ref[i, pl.ds(here, 1), :] for i in range(NZ)]
    top = lses[0]
    for i in range(1, NZ):
        top = jnp.maximum(top, lses[i])
    weights = [jnp.exp2((v - top) * SCALE2) for v in lses]
    total = weights[0]
    delta = weights[0] * stat_ref[0, pl.ds(HALF + here, 1), :]
    for i in range(1, NZ):
        total = total + weights[i]
        delta = delta + weights[i] * stat_ref[i, pl.ds(HALF + here, 1), :]
    lse = top + jnp.log2(total) * (1.0 / SCALE2)
    lse_ref[...] = lse
    delta_ref[...] = delta / total
    out_ref[...] = jnp.zeros(out_ref.shape, F32)
    dq_ref[...] = jnp.zeros(dq_ref.shape, F32)

    def slot(s):
        mark = slot_ref[1 + text * MAXT + s]
        owner = jnp.maximum(mark, 0)
        side = side_ref[jnp.where(mark < 0, SMP_DEV, owner)]
        k = slot_tokens(kv_ref, 0, s)
        v = slot_tokens(kv_ref, 1, s)
        sl = pl.ds(pl.multiple_of(owner * BL, BL), WIDE)
        sc = dot(jnp.concatenate([k, side], axis=1), qt_ref[:, sl], 1, 0)
        g = dot(v, dot_ref[:, sl], 1, 0)
        p = jnp.exp2((sc - lse_ref[:, sl]) * SCALE2)
        ds = (p * (g - delta_ref[:, sl])).astype(BF)
        p = p.astype(BF)
        out_ref[:, sl] += dot(v.T, p, 1, 0)
        dq_ref[:, sl] += dot(k.T, ds, 1, 0)
        dk = dot(ds, q_ref[sl], 1, 0) * SCALE
        dv = dot(p, do_ref[sl], 1, 0)
        dkv_ref[:, 0, s] = dk.astype(BF).reshape(TOKS // 8, 8, HD)
        dkv_ref[:, 1, s] = dv.astype(BF).reshape(TOKS // 8, 8, HD)

    for s in range(MAXT):
        slot(s)
    rows_ref[0, 0] = out_ref[...].astype(BF)
    rows_ref[0, 1] = (dq_ref[...] * SCALE).astype(BF)


def turn_kernel(rows_ref, out_ref, dq_ref):
    for j, ref in enumerate((out_ref, dq_ref)):
        for rb in range(RB):
            turned = rows_ref[0, j, :, rb * BL : (rb + 1) * BL].astype(F32).T.astype(BF)
            for h in range(HEADS):
                ref[rb * RBR : (rb + 1) * RBR, h * HD : (h + 1) * HD] = turned[
                    h * RBR : (h + 1) * RBR
                ]


def params(mib):
    return pltpu.CompilerParams(vmem_limit_bytes=mib * MIB)


def per_device(queries, keys, values, d_out, tile_sample, row_sample):
    z = lax.axis_index("z")
    c = lax.axis_index("c")
    tiles, patch, width = keys.shape
    plane = ("c", "tensor")

    mine = pl.pallas_call(
        pack_kernel,
        out_shape=jax.ShapeDtypeStruct((NQ + ROWS, LANES), BF),
        compiler_params=params(56),
        name="pack",
    )(row_sample, queries, d_out)
    pack = lax.all_gather(mine, "z", axis=0, tiled=False)

    owner = tile_sample // SMP_DEV
    ids = jnp.arange(tiles, dtype=jnp.int32)
    rank = jnp.sum(
        ((owner[:, None] == owner[None, :]) & (ids[None, :] < ids[:, None])).astype(jnp.int32),
        axis=1, dtype=jnp.int32,
    )
    spot = (owner % NC) * SLOTS + (owner // NC) * MAXT + rank
    match = spot[None, :] == jnp.arange(NC * SLOTS, dtype=jnp.int32)[:, None]
    spot_tile = jnp.sum(jnp.where(match, ids[None, :] + 1, 0), axis=1, dtype=jnp.int32) - 1
    spot_sample = (
        jnp.sum(jnp.where(match, (tile_sample % SMP_DEV)[None, :] + 1, 0), axis=1, dtype=jnp.int32) - 1
    )
    slot_info = jnp.concatenate(
        [z.astype(jnp.int32)[None], lax.dynamic_slice_in_dim(spot_sample, c * SLOTS, SLOTS)]
    )

    flat = lambda a: a.transpose(1, 0, 2).reshape(patch * tiles, width)
    depth = patch * tiles
    spots = NC * SLOTS
    pair = 2 * HD
    sent = pl.pallas_call(
        select_kernel,
        grid=(width // pair,),
        in_specs=[
            pl.BlockSpec((spots, 1), lambda i: (0, 0)),
            pl.BlockSpec((depth, pair), lambda i: (0, i)),
            pl.BlockSpec((depth, pair), lambda i: (0, i)),
        ],
        out_specs=pl.BlockSpec((NC, 2, 2, SLOTS * 8, HD), lambda i: (0, i, 0, 0, 0)),
        out_shape=jax.ShapeDtypeStruct((NC, KVH, 2, SLOTS * 8, HD), BF),
        scratch_shapes=[pltpu.VMEM((2, pair // HD, spots * 8, HD), F32)],
        compiler_params=params(56),
        name="select",
    )(spot_tile[:, None], flat(keys), flat(values))
    kv = lax.all_to_all(
        sent.reshape(NC * KVH, 2 * SLOTS * 8, HD), plane, 0, 0, tiled=True
    ).reshape(NC * KVH, 2, SLOTS, 8, HD)

    row_scratch = [
        pltpu.VMEM((LANES, HD), BF),
        pltpu.VMEM((LANES, HD), BF),
        pltpu.VMEM((2 * HD, LANES), BF),
        pltpu.VMEM((HD, LANES), BF),
        pltpu.VMEM((SMP_DEV + 1, TOKS, HD), BF),
        pltpu.VMEM((1, LANES), F32),
        pltpu.VMEM((1, LANES), F32),
    ]
    whole = pl.BlockSpec(memory_space=pltpu.VMEM)
    pack_specs = [
        pl.BlockSpec((1, NQ + ROWS, LANES), lambda i, *_, h=h: (h * HALF + i, 0, 0))
        for h in range(2)
    ]
    kv_specs = [
        pl.BlockSpec((NC * KVH, 2, MAXT, 8, HD), lambda i, *_, h=h: (0, 0, h * HALF + i, 0, 0))
        for h in range(2)
    ]
    parts = []
    for h in range(2):
        stat = pl.pallas_call(
            functools.partial(stats_kernel, h),
            grid_spec=pltpu.PrefetchScalarGridSpec(
                num_scalar_prefetch=1,
                grid=(HALF,),
                in_specs=[pack_specs[h], kv_specs[h]],
                out_specs=pl.BlockSpec((NZ, NZ, LANES), lambda i, *_: (0, 0, 0)),
                scratch_shapes=row_scratch + [pltpu.VMEM((1, LANES), F32)],
            ),
            out_shape=jax.ShapeDtypeStruct((NZ, NZ, LANES), F32),
            compiler_params=params(56),
            name=f"stats{h}",
        )(slot_info, pack, kv)
        parts.append(lax.all_to_all(stat, "z", 0, 0, tiled=True))

    made = []
    for h in range(2):
        made = pl.pallas_call(
            functools.partial(grad_kernel, h),
            grid_spec=pltpu.PrefetchScalarGridSpec(
                num_scalar_prefetch=1,
                grid=(HALF,),
                in_specs=[pack_specs[h], kv_specs[h], whole]
                + [pl.BlockSpec(memory_space=pl.ANY)] * len(made),
                out_specs=[
                    pl.BlockSpec((1, 2, HD, LANES), lambda i, *_, h=h: (h * HALF + i, 0, 0, 0)),
                    kv_specs[h],
                ],
                scratch_shapes=row_scratch + [pltpu.VMEM((HD, LANES), F32)] * 2,
            ),
            out_shape=[
                jax.ShapeDtypeStruct((NZ, 2, HD, LANES), BF),
                jax.ShapeDtypeStruct((NC * KVH, 2, SLOTS, 8, HD), BF),
            ],
            input_output_aliases={4 + j: j for j in range(len(made))},
            compiler_params=params(56),
            name=f"grads{h}",
        )(slot_info, pack, kv, parts[h], *made)
    rows, dkv = made

    home = lax.psum_scatter(rows, "z", scatter_dimension=0, tiled=True)
    returned = lax.all_to_all(
        dkv.reshape(NC * KVH, 2 * SLOTS * 8, HD), plane, 0, 0, tiled=True
    ).reshape(NC, KVH, 2, SLOTS * 8, HD)

    d_key, d_value = pl.pallas_call(
        return_kernel,
        grid=(KVH,),
        in_specs=[
            pl.BlockSpec((tiles, 1), lambda i: (0, 0)),
            pl.BlockSpec((NC, 1, 2, SLOTS * 8, HD), lambda i: (0, i, 0, 0, 0)),
        ],
        out_specs=[pl.BlockSpec((depth, HD), lambda i: (0, i))] * 2,
        out_shape=[jax.ShapeDtypeStruct((depth, width), BF)] * 2,
        scratch_shapes=[pltpu.VMEM((2, spots * 8, HD), F32)],
        compiler_params=params(32),
        name="give_back",
    )(spot[:, None], returned)
    unflat = lambda a: a.reshape(patch, tiles, width).transpose(1, 0, 2)

    attn_out, d_query = pl.pallas_call(
        turn_kernel,
        out_shape=[jax.ShapeDtypeStruct((ROWS, LANES), BF)] * 2,
        compiler_params=params(56),
        name="turn",
    )(home)
    return (attn_out, d_query, unflat(d_key), unflat(d_value))


def solution(mesh):
    split = Mesh(mesh.devices.reshape(NZ, NC, KVH), ("z", "c", "tensor"))
    rows = P(("z", "c"), "tensor")
    tokens = P(None, ("z", "c", "tensor"), None)
    return jax.shard_map(
        per_device,
        mesh=split,
        in_specs=(rows, tokens, tokens, rows, P(), P(("z", "c"), None)),
        out_specs=(rows, rows, tokens, tokens),
        check_vma=False,
    )
```

```python
import functools
import math

import jax
import jax.numpy as jnp
from jax import lax
from jax.experimental import pallas as pl
from jax.experimental.pallas import tpu as pltpu
from jax.sharding import Mesh
from jax.sharding import PartitionSpec as P

HD = 128
QH = 32
KVH = 4
PATCHES = 1601
SMP_DEV = 2
MAXT = 3
NZ = 8
NC = 8
ROWS = 128
HEADS = QH // KVH
RB = 4
RBR = ROWS // RB
BL = HEADS * RBR
LANES = HEADS * ROWS
SLOTS = NZ * MAXT
TOKS = 256
WIDE = (RB - 1) * BL
HALF = NZ // 2
NEG = -1e30
SCALE = 1.0 / math.sqrt(HD)
SCALE2 = SCALE / math.log(2.0)
BF = jnp.bfloat16
F32 = jnp.float32
MIB = 1024 * 1024


def dot(a, b, ca, cb):
    return lax.dot_general(a, b, (((ca,), (cb,)), ((), ())), preferred_element_type=F32)


def select_kernel(spot_ref, k_ref, v_ref, out_ref, rows_ref):
    spots = spot_ref.shape[0]
    tiles = k_ref.shape[0] // 7
    width = k_ref.shape[1]
    col = lax.broadcasted_iota(jnp.int32, (spots, tiles), 1)
    pick = jnp.where(col == spot_ref[...], 1.0, 0.0).astype(BF)
    for j, ref in enumerate((k_ref, v_ref)):
        for n in range(7):
            rows = dot(pick, ref[n * tiles : (n + 1) * tiles], 1, 0)
            for x in range(width // HD):
                rows_ref[j, x, pl.ds(n, spots, stride=8), :] = rows[:, x * HD : (x + 1) * HD]
        for x in range(width // HD):
            rows_ref[j, x, pl.ds(7, spots, stride=8), :] = jnp.zeros((spots, HD), F32)
            for c in range(NC):
                out_ref[c, x, j] = rows_ref[j, x, c * SLOTS * 8 : (c + 1) * SLOTS * 8].astype(BF)


def return_kernel(spot_ref, recv_ref, dk_ref, dv_ref, rows_ref):
    spots = NC * SLOTS
    tiles = spot_ref.shape[0]
    col = lax.broadcasted_iota(jnp.int32, (tiles, spots), 1)
    pick = jnp.where(col == spot_ref[...], 1.0, 0.0).astype(BF)
    for j in range(2):
        rows_ref[j] = recv_ref[:, 0, j].astype(F32).reshape(spots * 8, HD)
    for n in range(7):
        both = jnp.concatenate(
            [rows_ref[j, pl.ds(n, spots, stride=8), :].astype(BF) for j in range(2)], axis=1
        )
        rows = dot(pick, both, 1, 0).astype(BF)
        dk_ref[n * tiles : (n + 1) * tiles] = rows[:, :HD]
        dv_ref[n * tiles : (n + 1) * tiles] = rows[:, HD:]


def pack_kernel(q_ref, do_ref, out_ref):
    out_ref[:ROWS] = q_ref[...]
    out_ref[ROWS:] = do_ref[...]


def load_rows(first, pack_ref, q_ref, do_ref, qt_ref, dot_ref):
    for rb in range(RB):
        sl = slice(rb * BL, (rb + 1) * BL)
        for h in range(HEADS):
            lo = rb * BL + h * RBR
            cols = slice(h * HD, (h + 1) * HD)
            q_ref[lo : lo + RBR] = pack_ref[0, rb * RBR : (rb + 1) * RBR, cols]
            do_ref[lo : lo + RBR] = pack_ref[0, ROWS + rb * RBR : ROWS + (rb + 1) * RBR, cols]
        qt_ref[0:HD, sl] = q_ref[sl].T
        dot_ref[:, sl] = do_ref[sl].T
    lane = lax.broadcasted_iota(jnp.int32, (16, LANES), 1)
    second = (lane // BL) * RBR + lane % RBR >= first
    row = lax.broadcasted_iota(jnp.int32, (16, LANES), 0)
    off = jnp.where(
        row == 0, 1.0,
        jnp.where(((row == 1) & second) | ((row == 2) & ~second), NEG, 0.0),
    )
    qt_ref[HD : HD + 16] = off.astype(BF)


def set_up(z, qt_ref, side_ref):
    qt_ref[HD:] = jnp.zeros((HD, LANES), BF)
    i = lax.broadcasted_iota(jnp.int32, (TOKS, HD), 0)
    lane = lax.broadcasted_iota(jnp.int32, (TOKS, HD), 1)
    n = i % 8
    pos = z * 224 + (i // 8) * 7 + n
    empty = (n >= 7) | (pos >= PATCHES)
    for j in range(SMP_DEV + 1):
        none = empty if j < SMP_DEV else lane >= 0
        side_ref[j] = jnp.where(
            lane == 0, jnp.where(none, NEG, 0.0), jnp.where(lane == 1 + j, 1.0, 0.0)
        ).astype(BF)


def slot_tokens(kv_ref, j, s):
    return kv_ref[:, j, s].reshape(TOKS, HD)


def stats_kernel(half, slot_ref, pack_ref, kv_ref, stat_ref,
                 q_ref, do_ref, qt_ref, dot_ref, side_ref, m_ref, l_ref, d_ref):
    here = pl.program_id(0)
    text = half * HALF + here

    @pl.when(here == 0)
    def _():
        set_up(slot_ref[0], qt_ref, side_ref)

    load_rows(slot_ref[1 + SLOTS + text], pack_ref, q_ref, do_ref, qt_ref, dot_ref)
    m_ref[...] = jnp.full(m_ref.shape, 2 * NEG, F32)
    l_ref[...] = jnp.zeros(l_ref.shape, F32)
    d_ref[...] = jnp.zeros(d_ref.shape, F32)

    def slot(s):
        mark = slot_ref[1 + text * MAXT + s]
        owner = jnp.maximum(mark, 0)
        side = side_ref[jnp.where(mark < 0, SMP_DEV, owner)]
        k = jnp.concatenate([slot_tokens(kv_ref, 0, s), side], axis=1)
        v = slot_tokens(kv_ref, 1, s)
        sl = pl.ds(pl.multiple_of(owner * BL, BL), WIDE)
        sc = dot(k, qt_ref[:, sl], 1, 0)
        g = dot(v, dot_ref[:, sl], 1, 0)
        top = jnp.max(sc, axis=0, keepdims=True)
        p = jnp.exp2((sc - top) * SCALE2)
        total = jnp.sum(p, axis=0, keepdims=True)
        delta = jnp.sum(p * g, axis=0, keepdims=True)
        old = m_ref[:, sl]
        new = jnp.maximum(old, top)
        a = jnp.exp2((old - new) * SCALE2)
        b = jnp.exp2((top - new) * SCALE2)
        m_ref[:, sl] = new
        l_ref[:, sl] = l_ref[:, sl] * a + total * b
        d_ref[:, sl] = d_ref[:, sl] * a + delta * b

    for s in range(MAXT):
        slot(s)
    lse = m_ref[...] + jnp.log2(l_ref[...]) * (1.0 / SCALE2)
    delta = d_ref[...] / l_ref[...]
    for i in range(NZ):
        stat_ref[i, pl.ds(here, 1), :] = lse
        stat_ref[i, pl.ds(HALF + here, 1), :] = delta


def grad_kernel(half, slot_ref, pack_ref, kv_ref, stat_ref, *refs):
    (rows_ref, dkv_ref, q_ref, do_ref, qt_ref, dot_ref, side_ref,
     lse_ref, delta_ref, dq_ref, out_ref) = refs[2 * half :]
    here = pl.program_id(0)
    text = half * HALF + here

    @pl.when(here == 0)
    def _():
        set_up(slot_ref[0], qt_ref, side_ref)

    load_rows(slot_ref[1 + SLOTS + text], pack_ref, q_ref, do_ref, qt_ref, dot_ref)
    lses = [stat_ref[i, pl.ds(here, 1), :] for i in range(NZ)]
    top = lses[0]
    for i in range(1, NZ):
        top = jnp.maximum(top, lses[i])
    weights = [jnp.exp2((v - top) * SCALE2) for v in lses]
    total = weights[0]
    delta = weights[0] * stat_ref[0, pl.ds(HALF + here, 1), :]
    for i in range(1, NZ):
        total = total + weights[i]
        delta = delta + weights[i] * stat_ref[i, pl.ds(HALF + here, 1), :]
    lse = top + jnp.log2(total) * (1.0 / SCALE2)
    lse_ref[...] = lse
    delta_ref[...] = delta / total
    out_ref[...] = jnp.zeros(out_ref.shape, F32)
    dq_ref[...] = jnp.zeros(dq_ref.shape, F32)

    def slot(s):
        mark = slot_ref[1 + text * MAXT + s]
        owner = jnp.maximum(mark, 0)
        side = side_ref[jnp.where(mark < 0, SMP_DEV, owner)]
        k = slot_tokens(kv_ref, 0, s)
        v = slot_tokens(kv_ref, 1, s)
        sl = pl.ds(pl.multiple_of(owner * BL, BL), WIDE)
        sc = dot(jnp.concatenate([k, side], axis=1), qt_ref[:, sl], 1, 0)
        g = dot(v, dot_ref[:, sl], 1, 0)
        p = jnp.exp2((sc - lse_ref[:, sl]) * SCALE2)
        ds = (p * (g - delta_ref[:, sl])).astype(BF)
        p = p.astype(BF)
        out_ref[:, sl] += dot(v.T, p, 1, 0)
        dq_ref[:, sl] += dot(k.T, ds, 1, 0)
        dk = dot(ds, q_ref[sl], 1, 0) * SCALE
        dv = dot(p, do_ref[sl], 1, 0)
        dkv_ref[:, 0, s] = dk.astype(BF).reshape(TOKS // 8, 8, HD)
        dkv_ref[:, 1, s] = dv.astype(BF).reshape(TOKS // 8, 8, HD)

    for s in range(MAXT):
        slot(s)
    rows_ref[0, 0] = out_ref[...].astype(BF)
    rows_ref[0, 1] = (dq_ref[...] * SCALE).astype(BF)


def turn_kernel(rows_ref, out_ref, dq_ref):
    for j, ref in enumerate((out_ref, dq_ref)):
        for rb in range(RB):
            turned = rows_ref[0, j, :, rb * BL : (rb + 1) * BL].astype(F32).T.astype(BF)
            for h in range(HEADS):
                ref[rb * RBR : (rb + 1) * RBR, h * HD : (h + 1) * HD] = turned[
                    h * RBR : (h + 1) * RBR
                ]


def params(mib):
    return pltpu.CompilerParams(vmem_limit_bytes=mib * MIB)


def per_device(queries, keys, values, d_out, tile_sample, row_sample):
    z = lax.axis_index("z")
    c = lax.axis_index("c")
    tiles, patch, width = keys.shape
    plane = ("c", "tensor")

    mine = pl.pallas_call(
        pack_kernel,
        out_shape=jax.ShapeDtypeStruct((2 * ROWS, LANES), BF),
        compiler_params=params(56),
        name="pack",
    )(queries, d_out)
    pack = lax.all_gather(mine, "z", axis=0, tiled=False)

    mine_first = jnp.sum(jnp.where(row_sample == 0, 1.0, 0.0), axis=1, keepdims=True)
    mine_first = jnp.broadcast_to(mine_first, (1, HD))
    firsts = [mine_first] + [
        lax.ppermute(mine_first, "z", [(i, (i + by) % NZ) for i in range(NZ)])
        for by in range(1, NZ)
    ]
    back = (z - jnp.arange(NZ, dtype=jnp.int32) + NZ) % NZ
    firsts = jnp.concatenate(firsts, axis=0)[:, 0]
    firsts = jnp.sum(
        jnp.where(back[:, None] == jnp.arange(NZ, dtype=jnp.int32)[None, :], firsts[:, None], 0.0),
        axis=0,
    ).astype(jnp.int32)

    owner = tile_sample // SMP_DEV
    ids = jnp.arange(tiles, dtype=jnp.int32)
    rank = jnp.sum(
        ((owner[:, None] == owner[None, :]) & (ids[None, :] < ids[:, None])).astype(jnp.int32),
        axis=1, dtype=jnp.int32,
    )
    spot = (owner % NC) * SLOTS + (owner // NC) * MAXT + rank
    match = spot[None, :] == jnp.arange(NC * SLOTS, dtype=jnp.int32)[:, None]
    spot_tile = jnp.sum(jnp.where(match, ids[None, :] + 1, 0), axis=1, dtype=jnp.int32) - 1
    spot_sample = (
        jnp.sum(jnp.where(match, (tile_sample % SMP_DEV)[None, :] + 1, 0), axis=1, dtype=jnp.int32) - 1
    )
    slot_info = jnp.concatenate(
        [z.astype(jnp.int32)[None], lax.dynamic_slice_in_dim(spot_sample, c * SLOTS, SLOTS), firsts]
    )

    flat = lambda a: a.transpose(1, 0, 2).reshape(patch * tiles, width)
    depth = patch * tiles
    spots = NC * SLOTS
    pair = 2 * HD
    sent = pl.pallas_call(
        select_kernel,
        grid=(width // pair,),
        in_specs=[
            pl.BlockSpec((spots, 1), lambda i: (0, 0)),
            pl.BlockSpec((depth, pair), lambda i: (0, i)),
            pl.BlockSpec((depth, pair), lambda i: (0, i)),
        ],
        out_specs=pl.BlockSpec((NC, 2, 2, SLOTS * 8, HD), lambda i: (0, i, 0, 0, 0)),
        out_shape=jax.ShapeDtypeStruct((NC, KVH, 2, SLOTS * 8, HD), BF),
        scratch_shapes=[pltpu.VMEM((2, pair // HD, spots * 8, HD), F32)],
        compiler_params=params(56),
        name="select",
    )(spot_tile[:, None], flat(keys), flat(values))
    kv = lax.all_to_all(
        sent.reshape(NC * KVH, 2 * SLOTS * 8, HD), plane, 0, 0, tiled=True
    ).reshape(NC * KVH, 2, SLOTS, 8, HD)

    row_scratch = [
        pltpu.VMEM((LANES, HD), BF),
        pltpu.VMEM((LANES, HD), BF),
        pltpu.VMEM((2 * HD, LANES), BF),
        pltpu.VMEM((HD, LANES), BF),
        pltpu.VMEM((SMP_DEV + 1, TOKS, HD), BF),
        pltpu.VMEM((1, LANES), F32),
        pltpu.VMEM((1, LANES), F32),
    ]
    whole = pl.BlockSpec(memory_space=pltpu.VMEM)
    pack_specs = [
        pl.BlockSpec((1, 2 * ROWS, LANES), lambda i, *_, h=h: (h * HALF + i, 0, 0))
        for h in range(2)
    ]
    kv_specs = [
        pl.BlockSpec((NC * KVH, 2, MAXT, 8, HD), lambda i, *_, h=h: (0, 0, h * HALF + i, 0, 0))
        for h in range(2)
    ]
    parts = []
    for h in range(2):
        stat = pl.pallas_call(
            functools.partial(stats_kernel, h),
            grid_spec=pltpu.PrefetchScalarGridSpec(
                num_scalar_prefetch=1,
                grid=(HALF,),
                in_specs=[pack_specs[h], kv_specs[h]],
                out_specs=pl.BlockSpec((NZ, NZ, LANES), lambda i, *_: (0, 0, 0)),
                scratch_shapes=row_scratch + [pltpu.VMEM((1, LANES), F32)],
            ),
            out_shape=jax.ShapeDtypeStruct((NZ, NZ, LANES), F32),
            compiler_params=params(56),
            name=f"stats{h}",
        )(slot_info, pack, kv)
        parts.append(lax.all_to_all(stat, "z", 0, 0, tiled=True))

    made = []
    for h in range(2):
        made = pl.pallas_call(
            functools.partial(grad_kernel, h),
            grid_spec=pltpu.PrefetchScalarGridSpec(
                num_scalar_prefetch=1,
                grid=(HALF,),
                in_specs=[pack_specs[h], kv_specs[h], whole]
                + [pl.BlockSpec(memory_space=pl.ANY)] * len(made),
                out_specs=[
                    pl.BlockSpec((1, 2, HD, LANES), lambda i, *_, h=h: (h * HALF + i, 0, 0, 0)),
                    kv_specs[h],
                ],
                scratch_shapes=row_scratch + [pltpu.VMEM((HD, LANES), F32)] * 2,
            ),
            out_shape=[
                jax.ShapeDtypeStruct((NZ, 2, HD, LANES), BF),
                jax.ShapeDtypeStruct((NC * KVH, 2, SLOTS, 8, HD), BF),
            ],
            input_output_aliases={4 + j: j for j in range(len(made))},
            compiler_params=params(56),
            name=f"grads{h}",
        )(slot_info, pack, kv, parts[h], *made)
    rows, dkv = made

    home = lax.psum_scatter(rows, "z", scatter_dimension=0, tiled=True)
    returned = lax.all_to_all(
        dkv.reshape(NC * KVH, 2 * SLOTS * 8, HD), plane, 0, 0, tiled=True
    ).reshape(NC, KVH, 2, SLOTS * 8, HD)

    d_key, d_value = pl.pallas_call(
        return_kernel,
        grid=(KVH,),
        in_specs=[
            pl.BlockSpec((tiles, 1), lambda i: (0, 0)),
            pl.BlockSpec((NC, 1, 2, SLOTS * 8, HD), lambda i: (0, i, 0, 0, 0)),
        ],
        out_specs=[pl.BlockSpec((depth, HD), lambda i: (0, i))] * 2,
        out_shape=[jax.ShapeDtypeStruct((depth, width), BF)] * 2,
        scratch_shapes=[pltpu.VMEM((2, spots * 8, HD), F32)],
        compiler_params=params(32),
        name="give_back",
    )(spot[:, None], returned)
    unflat = lambda a: a.reshape(patch, tiles, width).transpose(1, 0, 2)

    attn_out, d_query = pl.pallas_call(
        turn_kernel,
        out_shape=[jax.ShapeDtypeStruct((ROWS, LANES), BF)] * 2,
        compiler_params=params(56),
        name="turn",
    )(home)
    return (attn_out, d_query, unflat(d_key), unflat(d_value))


def solution(mesh):
    split = Mesh(mesh.devices.reshape(NZ, NC, KVH), ("z", "c", "tensor"))
    rows = P(("z", "c"), "tensor")
    tokens = P(None, ("z", "c", "tensor"), None)
    return jax.shard_map(
        per_device,
        mesh=split,
        in_specs=(rows, tokens, tokens, rows, P(), P(("z", "c"), None)),
        out_specs=(rows, rows, tokens, tokens),
        check_vma=False,
    )
```

```python
import functools
import math

import jax
import jax.numpy as jnp
from jax import lax
from jax.experimental import pallas as pl
from jax.experimental.pallas import tpu as pltpu
from jax.sharding import Mesh
from jax.sharding import PartitionSpec as P

HD = 128
QH = 32
KVH = 4
PATCHES = 1601
SMP_DEV = 2
MAXT = 3
NZ = 8
NC = 8
ROWS = 128
HEADS = QH // KVH
RB = 4
RBR = ROWS // RB
BL = HEADS * RBR
LANES = HEADS * ROWS
SLOTS = NZ * MAXT
TOKS = 256
WIDE = (RB - 1) * BL
HALF = NZ // 2
NEG = -1e30
SCALE = 1.0 / math.sqrt(HD)
SCALE2 = SCALE / math.log(2.0)
BF = jnp.bfloat16
F32 = jnp.float32
MIB = 1024 * 1024


def dot(a, b, ca, cb):
    return lax.dot_general(a, b, (((ca,), (cb,)), ((), ())), preferred_element_type=F32)


def select_kernel(spot_ref, k_ref, v_ref, out_ref, rows_ref):
    spots = spot_ref.shape[0]
    tiles = k_ref.shape[0] // 7
    width = k_ref.shape[1]
    col = lax.broadcasted_iota(jnp.int32, (spots, tiles), 1)
    pick = jnp.where(col == spot_ref[...], 1.0, 0.0).astype(BF)
    for j, ref in enumerate((k_ref, v_ref)):
        for n in range(7):
            rows = dot(pick, ref[n * tiles : (n + 1) * tiles], 1, 0)
            for x in range(width // HD):
                rows_ref[j, x, pl.ds(n, spots, stride=8), :] = rows[:, x * HD : (x + 1) * HD]
        for x in range(width // HD):
            rows_ref[j, x, pl.ds(7, spots, stride=8), :] = jnp.zeros((spots, HD), F32)
            for c in range(NC):
                out_ref[c, x, j] = rows_ref[j, x, c * SLOTS * 8 : (c + 1) * SLOTS * 8].astype(BF)


def return_kernel(spot_ref, recv_ref, dk_ref, dv_ref, rows_ref):
    spots = NC * SLOTS
    tiles = spot_ref.shape[0]
    col = lax.broadcasted_iota(jnp.int32, (tiles, spots), 1)
    pick = jnp.where(col == spot_ref[...], 1.0, 0.0).astype(BF)
    for j in range(2):
        rows_ref[j] = recv_ref[:, 0, j].astype(F32).reshape(spots * 8, HD)
    for n in range(7):
        both = jnp.concatenate(
            [rows_ref[j, pl.ds(n, spots, stride=8), :].astype(BF) for j in range(2)], axis=1
        )
        rows = dot(pick, both, 1, 0).astype(BF)
        dk_ref[n * tiles : (n + 1) * tiles] = rows[:, :HD]
        dv_ref[n * tiles : (n + 1) * tiles] = rows[:, HD:]


def pack_kernel(q_ref, do_ref, out_ref):
    out_ref[:ROWS] = q_ref[...]
    out_ref[ROWS:] = do_ref[...]


def load_rows(first, pack_ref, q_ref, do_ref, qt_ref, dot_ref):
    for rb in range(RB):
        sl = slice(rb * BL, (rb + 1) * BL)
        for h in range(HEADS):
            lo = rb * BL + h * RBR
            cols = slice(h * HD, (h + 1) * HD)
            q_ref[lo : lo + RBR] = pack_ref[0, rb * RBR : (rb + 1) * RBR, cols]
            do_ref[lo : lo + RBR] = pack_ref[0, ROWS + rb * RBR : ROWS + (rb + 1) * RBR, cols]
        qt_ref[0:HD, sl] = q_ref[sl].T
        dot_ref[:, sl] = do_ref[sl].T
    lane = lax.broadcasted_iota(jnp.int32, (16, LANES), 1)
    second = (lane // BL) * RBR + lane % RBR >= first
    row = lax.broadcasted_iota(jnp.int32, (16, LANES), 0)
    off = jnp.where(
        row == 0, 1.0,
        jnp.where(((row == 1) & second) | ((row == 2) & ~second), NEG, 0.0),
    )
    qt_ref[HD : HD + 16] = off.astype(BF)


def set_up(z, qt_ref, side_ref):
    qt_ref[HD:] = jnp.zeros((HD, LANES), BF)
    i = lax.broadcasted_iota(jnp.int32, (TOKS, HD), 0)
    lane = lax.broadcasted_iota(jnp.int32, (TOKS, HD), 1)
    n = i % 8
    pos = z * 224 + (i // 8) * 7 + n
    empty = (n >= 7) | (pos >= PATCHES)
    for j in range(SMP_DEV + 1):
        none = empty if j < SMP_DEV else lane >= 0
        side_ref[j] = jnp.where(
            lane == 0, jnp.where(none, NEG, 0.0), jnp.where(lane == 1 + j, 1.0, 0.0)
        ).astype(BF)


def slot_tokens(kv_ref, j, s):
    return kv_ref[:, j, s].reshape(TOKS, HD)


def stats_kernel(half, slot_ref, pack_ref, kv_ref, stat_ref,
                 q_ref, do_ref, qt_ref, dot_ref, side_ref, m_ref, l_ref, d_ref):
    here = pl.program_id(0)
    text = half * HALF + here

    @pl.when(here == 0)
    def _():
        set_up(slot_ref[0], qt_ref, side_ref)

    load_rows(slot_ref[1 + SLOTS + text], pack_ref, q_ref, do_ref, qt_ref, dot_ref)
    m_ref[...] = jnp.full(m_ref.shape, 2 * NEG, F32)
    l_ref[...] = jnp.zeros(l_ref.shape, F32)
    d_ref[...] = jnp.zeros(d_ref.shape, F32)

    def slot(s):
        mark = slot_ref[1 + text * MAXT + s]
        owner = jnp.maximum(mark, 0)
        side = side_ref[jnp.where(mark < 0, SMP_DEV, owner)]
        k = jnp.concatenate([slot_tokens(kv_ref, 0, s), side], axis=1)
        v = slot_tokens(kv_ref, 1, s)
        sl = pl.ds(pl.multiple_of(owner * BL, BL), WIDE)
        sc = dot(k, qt_ref[:, sl], 1, 0)
        g = dot(v, dot_ref[:, sl], 1, 0)
        top = jnp.max(sc, axis=0, keepdims=True)
        p = jnp.exp2((sc - top) * SCALE2)
        total = jnp.sum(p, axis=0, keepdims=True)
        delta = jnp.sum(p * g, axis=0, keepdims=True)
        old = m_ref[:, sl]
        new = jnp.maximum(old, top)
        a = jnp.exp2((old - new) * SCALE2)
        b = jnp.exp2((top - new) * SCALE2)
        m_ref[:, sl] = new
        l_ref[:, sl] = l_ref[:, sl] * a + total * b
        d_ref[:, sl] = d_ref[:, sl] * a + delta * b

    for s in range(MAXT):
        slot(s)
    lse = m_ref[...] + jnp.log2(l_ref[...]) * (1.0 / SCALE2)
    delta = d_ref[...] / l_ref[...]
    for i in range(NZ):
        stat_ref[i, pl.ds(here, 1), :] = lse
        stat_ref[i, pl.ds(HALF + here, 1), :] = delta


def grad_kernel(half, base, keep, aliased, slot_ref, pack_ref, kv_ref, stat_ref, *refs):
    refs = refs[aliased:]
    rows_ref = refs[0] if base == 0 else None
    dkv_ref = refs[1] if base == 0 else refs[0]
    (q_ref, do_ref, qt_ref, dot_ref, side_ref,
     lse_ref, delta_ref, dq_ref, out_ref, ds_ref, p_ref) = refs[-11:]
    here = pl.program_id(0)
    text = half * HALF + base + here

    @pl.when(here == 0)
    def _():
        set_up(slot_ref[0], qt_ref, side_ref)

    load_rows(slot_ref[1 + SLOTS + text], pack_ref, q_ref, do_ref, qt_ref, dot_ref)
    lses = [stat_ref[i, pl.ds(base + here, 1), :] for i in range(NZ)]
    top = lses[0]
    for i in range(1, NZ):
        top = jnp.maximum(top, lses[i])
    weights = [jnp.exp2((v - top) * SCALE2) for v in lses]
    total = weights[0]
    delta = weights[0] * stat_ref[0, pl.ds(HALF + base + here, 1), :]
    for i in range(1, NZ):
        total = total + weights[i]
        delta = delta + weights[i] * stat_ref[i, pl.ds(HALF + base + here, 1), :]
    lse = top + jnp.log2(total) * (1.0 / SCALE2)
    lse_ref[...] = lse
    delta_ref[...] = delta / total
    out_ref[...] = jnp.zeros(out_ref.shape, F32)
    dq_ref[...] = jnp.zeros(dq_ref.shape, F32)

    def slot(s):
        mark = slot_ref[1 + text * MAXT + s]
        owner = jnp.maximum(mark, 0)
        side = side_ref[jnp.where(mark < 0, SMP_DEV, owner)]
        k = slot_tokens(kv_ref, 0, s)
        v = slot_tokens(kv_ref, 1, s)
        sl = pl.ds(pl.multiple_of(owner * BL, BL), WIDE)
        sc = dot(jnp.concatenate([k, side], axis=1), qt_ref[:, sl], 1, 0)
        g = dot(v, dot_ref[:, sl], 1, 0)
        p = jnp.exp2((sc - lse_ref[:, sl]) * SCALE2)
        ds = (p * (g - delta_ref[:, sl])).astype(BF)
        p = p.astype(BF)
        if rows_ref is not None:
            out_ref[:, sl] += dot(v.T, p, 1, 0)
            dq_ref[:, sl] += dot(k.T, ds, 1, 0)
        if keep is None:
            tokens(s, sl, ds, p)
        else:
            ds_ref[s] = ds
            p_ref[s] = p

    def tokens(s, sl, ds, p):
        dk = dot(ds, q_ref[sl], 1, 0) * SCALE
        dv = dot(p, do_ref[sl], 1, 0)
        dkv_ref[:, 0, s] = dk.astype(BF).reshape(TOKS // 8, 8, HD)
        dkv_ref[:, 1, s] = dv.astype(BF).reshape(TOKS // 8, 8, HD)

    for s in range(MAXT):
        slot(s)
    if rows_ref is not None:
        rows_ref[0, 0] = out_ref[...].astype(BF)
        rows_ref[0, 1] = (dq_ref[...] * SCALE).astype(BF)
    if keep is not None:

        @pl.when(here < keep)
        def _():
            for s in range(MAXT):
                owner = jnp.maximum(slot_ref[1 + text * MAXT + s], 0)
                sl = pl.ds(pl.multiple_of(owner * BL, BL), WIDE)
                tokens(s, sl, ds_ref[s], p_ref[s])


def turn_kernel(rows_ref, out_ref, dq_ref):
    for j, ref in enumerate((out_ref, dq_ref)):
        for rb in range(RB):
            turned = rows_ref[0, j, :, rb * BL : (rb + 1) * BL].astype(F32).T.astype(BF)
            for h in range(HEADS):
                ref[rb * RBR : (rb + 1) * RBR, h * HD : (h + 1) * HD] = turned[
                    h * RBR : (h + 1) * RBR
                ]


def params(mib):
    return pltpu.CompilerParams(vmem_limit_bytes=mib * MIB)


def per_device(queries, keys, values, d_out, tile_sample, row_sample):
    z = lax.axis_index("z")
    c = lax.axis_index("c")
    tiles, patch, width = keys.shape
    plane = ("c", "tensor")

    mine = pl.pallas_call(
        pack_kernel,
        out_shape=jax.ShapeDtypeStruct((2 * ROWS, LANES), BF),
        compiler_params=params(56),
        name="pack",
    )(queries, d_out)
    pack = lax.all_gather(mine, "z", axis=0, tiled=False)

    mine_first = jnp.sum(jnp.where(row_sample == 0, 1.0, 0.0), axis=1, keepdims=True)
    mine_first = jnp.broadcast_to(mine_first, (1, HD))
    firsts = [mine_first] + [
        lax.ppermute(mine_first, "z", [(i, (i + by) % NZ) for i in range(NZ)])
        for by in range(1, NZ)
    ]
    back = (z - jnp.arange(NZ, dtype=jnp.int32) + NZ) % NZ
    firsts = jnp.concatenate(firsts, axis=0)[:, 0]
    firsts = jnp.sum(
        jnp.where(back[:, None] == jnp.arange(NZ, dtype=jnp.int32)[None, :], firsts[:, None], 0.0),
        axis=0,
    ).astype(jnp.int32)

    owner = tile_sample // SMP_DEV
    ids = jnp.arange(tiles, dtype=jnp.int32)
    rank = jnp.sum(
        ((owner[:, None] == owner[None, :]) & (ids[None, :] < ids[:, None])).astype(jnp.int32),
        axis=1, dtype=jnp.int32,
    )
    spot = (owner % NC) * SLOTS + (owner // NC) * MAXT + rank
    match = spot[None, :] == jnp.arange(NC * SLOTS, dtype=jnp.int32)[:, None]
    spot_tile = jnp.sum(jnp.where(match, ids[None, :] + 1, 0), axis=1, dtype=jnp.int32) - 1
    spot_sample = (
        jnp.sum(jnp.where(match, (tile_sample % SMP_DEV)[None, :] + 1, 0), axis=1, dtype=jnp.int32) - 1
    )
    slot_info = jnp.concatenate(
        [z.astype(jnp.int32)[None], lax.dynamic_slice_in_dim(spot_sample, c * SLOTS, SLOTS), firsts]
    )

    flat = lambda a: a.transpose(1, 0, 2).reshape(patch * tiles, width)
    depth = patch * tiles
    spots = NC * SLOTS
    pair = 2 * HD
    sent = pl.pallas_call(
        select_kernel,
        grid=(width // pair,),
        in_specs=[
            pl.BlockSpec((spots, 1), lambda i: (0, 0)),
            pl.BlockSpec((depth, pair), lambda i: (0, i)),
            pl.BlockSpec((depth, pair), lambda i: (0, i)),
        ],
        out_specs=pl.BlockSpec((NC, 2, 2, SLOTS * 8, HD), lambda i: (0, i, 0, 0, 0)),
        out_shape=jax.ShapeDtypeStruct((NC, KVH, 2, SLOTS * 8, HD), BF),
        scratch_shapes=[pltpu.VMEM((2, pair // HD, spots * 8, HD), F32)],
        compiler_params=params(56),
        name="select",
    )(spot_tile[:, None], flat(keys), flat(values))
    kv = lax.all_to_all(
        sent.reshape(NC * KVH, 2 * SLOTS * 8, HD), plane, 0, 0, tiled=True
    ).reshape(NC * KVH, 2, SLOTS, 8, HD)

    row_scratch = [
        pltpu.VMEM((LANES, HD), BF),
        pltpu.VMEM((LANES, HD), BF),
        pltpu.VMEM((2 * HD, LANES), BF),
        pltpu.VMEM((HD, LANES), BF),
        pltpu.VMEM((SMP_DEV + 1, TOKS, HD), BF),
        pltpu.VMEM((1, LANES), F32),
        pltpu.VMEM((1, LANES), F32),
    ]
    whole = pl.BlockSpec(memory_space=pltpu.VMEM)
    pack_specs = [
        pl.BlockSpec((1, 2 * ROWS, LANES), lambda i, *_, h=h: (h * HALF + i, 0, 0))
        for h in range(2)
    ]
    kv_specs = [
        pl.BlockSpec((NC * KVH, 2, MAXT, 8, HD), lambda i, *_, h=h: (0, 0, h * HALF + i, 0, 0))
        for h in range(2)
    ]
    parts = []
    for h in range(2):
        stat = pl.pallas_call(
            functools.partial(stats_kernel, h),
            grid_spec=pltpu.PrefetchScalarGridSpec(
                num_scalar_prefetch=1,
                grid=(HALF,),
                in_specs=[pack_specs[h], kv_specs[h]],
                out_specs=pl.BlockSpec((NZ, NZ, LANES), lambda i, *_: (0, 0, 0)),
                scratch_shapes=row_scratch + [pltpu.VMEM((1, LANES), F32)],
            ),
            out_shape=jax.ShapeDtypeStruct((NZ, NZ, LANES), F32),
            compiler_params=params(56),
            name=f"stats{h}",
        )(slot_info, pack, kv)
        parts.append(lax.all_to_all(stat, "z", 0, 0, tiled=True))

    rows_shape = jax.ShapeDtypeStruct((NZ, 2, HD, LANES), BF)
    dkv_shape = jax.ShapeDtypeStruct((NC * KVH, 2, SLOTS, 8, HD), BF)

    def grads(h, base, keep, made):
        first = h * HALF + base
        last = HALF - 1 if keep is None else keep - 1
        kv_block = (NC * KVH, 2, MAXT, 8, HD)
        rows_out = pl.BlockSpec((1, 2, HD, LANES), lambda i, *_: (first + i, 0, 0, 0))
        dkv_out = pl.BlockSpec(
            kv_block, lambda i, *_: (0, 0, first + jnp.minimum(i, last), 0, 0)
        )
        return pl.pallas_call(
            functools.partial(grad_kernel, h, base, keep, len(made)),
            grid_spec=pltpu.PrefetchScalarGridSpec(
                num_scalar_prefetch=1,
                grid=(HALF - base,),
                in_specs=[
                    pl.BlockSpec((1, 2 * ROWS, LANES), lambda i, *_: (first + i, 0, 0)),
                    pl.BlockSpec(kv_block, lambda i, *_: (0, 0, first + i, 0, 0)),
                    pl.BlockSpec((NZ, NZ, LANES), lambda i, *_: (0, 0, 0)),
                ]
                + [pl.BlockSpec(memory_space=pl.ANY)] * len(made),
                out_specs=[rows_out, dkv_out] if base == 0 else [dkv_out],
                scratch_shapes=row_scratch
                + [pltpu.VMEM((HD, LANES), F32)] * 2
                + [pltpu.VMEM((MAXT, TOKS, WIDE), BF)] * 2,
            ),
            out_shape=[rows_shape, dkv_shape] if base == 0 else [dkv_shape],
            input_output_aliases={4 + j: j for j in range(len(made))},
            compiler_params=params(56),
            name=f"grads{h}{base}",
        )(slot_info, pack, kv, parts[h], *made)

    made = grads(0, 0, None, ())
    rows, dkv = grads(1, 0, HALF // 2, made)
    (dkv,) = grads(1, HALF // 2, None, (dkv,))
    home = lax.psum_scatter(rows, "z", scatter_dimension=0, tiled=True)
    returned = lax.all_to_all(
        dkv.reshape(NC * KVH, 2 * SLOTS * 8, HD), plane, 0, 0, tiled=True
    ).reshape(NC, KVH, 2, SLOTS * 8, HD)

    d_key, d_value = pl.pallas_call(
        return_kernel,
        grid=(KVH,),
        in_specs=[
            pl.BlockSpec((tiles, 1), lambda i: (0, 0)),
            pl.BlockSpec((NC, 1, 2, SLOTS * 8, HD), lambda i: (0, i, 0, 0, 0)),
        ],
        out_specs=[pl.BlockSpec((depth, HD), lambda i: (0, i))] * 2,
        out_shape=[jax.ShapeDtypeStruct((depth, width), BF)] * 2,
        scratch_shapes=[pltpu.VMEM((2, spots * 8, HD), F32)],
        compiler_params=params(32),
        name="give_back",
    )(spot[:, None], returned)
    unflat = lambda a: a.reshape(patch, tiles, width).transpose(1, 0, 2)

    attn_out, d_query = pl.pallas_call(
        turn_kernel,
        out_shape=[jax.ShapeDtypeStruct((ROWS, LANES), BF)] * 2,
        compiler_params=params(56),
        name="turn",
    )(home)
    return (attn_out, d_query, unflat(d_key), unflat(d_value))


def solution(mesh):
    split = Mesh(mesh.devices.reshape(NZ, NC, KVH), ("z", "c", "tensor"))
    rows = P(("z", "c"), "tensor")
    tokens = P(None, ("z", "c", "tensor"), None)
    return jax.shard_map(
        per_device,
        mesh=split,
        in_specs=(rows, tokens, tokens, rows, P(), P(("z", "c"), None)),
        out_specs=(rows, rows, tokens, tokens),
        check_vma=False,
    )
```

```python
import functools
import math

import jax
import jax.numpy as jnp
from jax import lax
from jax.experimental import pallas as pl
from jax.experimental.pallas import tpu as pltpu
from jax.sharding import Mesh
from jax.sharding import PartitionSpec as P

HD = 128
QH = 32
KVH = 4
PATCHES = 1601
SMP_DEV = 2
MAXT = 3
NZ = 8
NC = 8
ROWS = 128
HEADS = QH // KVH
RB = 4
RBR = ROWS // RB
BL = HEADS * RBR
LANES = HEADS * ROWS
SLOTS = NZ * MAXT
TOKS = 256
WIDE = (RB - 1) * BL
HALF = NZ // 2
NEG = -1e30
SCALE = 1.0 / math.sqrt(HD)
SCALE2 = SCALE / math.log(2.0)
BF = jnp.bfloat16
F32 = jnp.float32
MIB = 1024 * 1024


def dot(a, b, ca, cb):
    return lax.dot_general(a, b, (((ca,), (cb,)), ((), ())), preferred_element_type=F32)


def select_kernel(spot_ref, k_ref, v_ref, out_ref, rows_ref):
    spots = spot_ref.shape[0]
    tiles = k_ref.shape[0] // 7
    width = k_ref.shape[1]
    col = lax.broadcasted_iota(jnp.int32, (spots, tiles), 1)
    pick = jnp.where(col == spot_ref[...], 1.0, 0.0).astype(BF)
    for j, ref in enumerate((k_ref, v_ref)):
        for n in range(7):
            rows = dot(pick, ref[n * tiles : (n + 1) * tiles], 1, 0)
            for x in range(width // HD):
                rows_ref[j, x, pl.ds(n, spots, stride=8), :] = rows[:, x * HD : (x + 1) * HD]
        for x in range(width // HD):
            rows_ref[j, x, pl.ds(7, spots, stride=8), :] = jnp.zeros((spots, HD), F32)
            for c in range(NC):
                out_ref[c, x, j] = rows_ref[j, x, c * SLOTS * 8 : (c + 1) * SLOTS * 8].astype(BF)


def return_kernel(spot_ref, recv_ref, dk_ref, dv_ref, rows_ref):
    spots = NC * SLOTS
    tiles = spot_ref.shape[0]
    col = lax.broadcasted_iota(jnp.int32, (tiles, spots), 1)
    pick = jnp.where(col == spot_ref[...], 1.0, 0.0).astype(BF)
    for j in range(2):
        rows_ref[j] = recv_ref[:, 0, j].astype(F32).reshape(spots * 8, HD)
    for n in range(7):
        both = jnp.concatenate(
            [rows_ref[j, pl.ds(n, spots, stride=8), :].astype(BF) for j in range(2)], axis=1
        )
        rows = dot(pick, both, 1, 0).astype(BF)
        dk_ref[n * tiles : (n + 1) * tiles] = rows[:, :HD]
        dv_ref[n * tiles : (n + 1) * tiles] = rows[:, HD:]


def pack_kernel(q_ref, do_ref, out_ref):
    @pl.when(pl.program_id(0) == 0)
    def _():
        out_ref[...] = q_ref[...]

    @pl.when(pl.program_id(0) == 1)
    def _():
        out_ref[...] = do_ref[...]


def load_rows(first, pack_ref, q_ref, do_ref, qt_ref, dot_ref):
    for rb in range(RB):
        sl = slice(rb * BL, (rb + 1) * BL)
        for h in range(HEADS):
            lo = rb * BL + h * RBR
            cols = slice(h * HD, (h + 1) * HD)
            q_ref[lo : lo + RBR] = pack_ref[0, rb * RBR : (rb + 1) * RBR, cols]
            do_ref[lo : lo + RBR] = pack_ref[0, ROWS + rb * RBR : ROWS + (rb + 1) * RBR, cols]
        qt_ref[0:HD, sl] = q_ref[sl].T
        dot_ref[:, sl] = do_ref[sl].T
    lane = lax.broadcasted_iota(jnp.int32, (16, LANES), 1)
    second = (lane // BL) * RBR + lane % RBR >= first
    row = lax.broadcasted_iota(jnp.int32, (16, LANES), 0)
    off = jnp.where(
        row == 0, 1.0,
        jnp.where(((row == 1) & second) | ((row == 2) & ~second), NEG, 0.0),
    )
    qt_ref[HD : HD + 16] = off.astype(BF)


def set_up(z, qt_ref, side_ref):
    qt_ref[HD:] = jnp.zeros((HD, LANES), BF)
    i = lax.broadcasted_iota(jnp.int32, (TOKS, HD), 0)
    lane = lax.broadcasted_iota(jnp.int32, (TOKS, HD), 1)
    n = i % 8
    pos = z * 224 + (i // 8) * 7 + n
    empty = (n >= 7) | (pos >= PATCHES)
    for j in range(SMP_DEV + 1):
        none = empty if j < SMP_DEV else lane >= 0
        side_ref[j] = jnp.where(
            lane == 0, jnp.where(none, NEG, 0.0), jnp.where(lane == 1 + j, 1.0, 0.0)
        ).astype(BF)


def slot_tokens(kv_ref, j, s):
    return kv_ref[:, j, s].reshape(TOKS, HD)


def stats_kernel(half, slot_ref, pack_ref, kv_ref, stat_ref,
                 q_ref, do_ref, qt_ref, dot_ref, side_ref, m_ref, l_ref, d_ref):
    here = pl.program_id(0)
    text = half * HALF + here

    @pl.when(here == 0)
    def _():
        set_up(slot_ref[0], qt_ref, side_ref)

    load_rows(slot_ref[1 + SLOTS + text], pack_ref, q_ref, do_ref, qt_ref, dot_ref)
    m_ref[...] = jnp.full(m_ref.shape, 2 * NEG, F32)
    l_ref[...] = jnp.zeros(l_ref.shape, F32)
    d_ref[...] = jnp.zeros(d_ref.shape, F32)

    def slot(s):
        mark = slot_ref[1 + text * MAXT + s]
        owner = jnp.maximum(mark, 0)
        side = side_ref[jnp.where(mark < 0, SMP_DEV, owner)]
        k = jnp.concatenate([slot_tokens(kv_ref, 0, s), side], axis=1)
        v = slot_tokens(kv_ref, 1, s)
        sl = pl.ds(pl.multiple_of(owner * BL, BL), WIDE)
        sc = dot(k, qt_ref[:, sl], 1, 0)
        g = dot(v, dot_ref[:, sl], 1, 0)
        top = jnp.max(sc, axis=0, keepdims=True)
        p = jnp.exp2((sc - top) * SCALE2)
        total = jnp.sum(p, axis=0, keepdims=True)
        delta = jnp.sum(p * g, axis=0, keepdims=True)
        old = m_ref[:, sl]
        new = jnp.maximum(old, top)
        a = jnp.exp2((old - new) * SCALE2)
        b = jnp.exp2((top - new) * SCALE2)
        m_ref[:, sl] = new
        l_ref[:, sl] = l_ref[:, sl] * a + total * b
        d_ref[:, sl] = d_ref[:, sl] * a + delta * b

    for s in range(MAXT):
        slot(s)
    lse = m_ref[...] + jnp.log2(l_ref[...]) * (1.0 / SCALE2)
    delta = d_ref[...] / l_ref[...]
    for i in range(NZ):
        stat_ref[i, pl.ds(here, 1), :] = lse
        stat_ref[i, pl.ds(HALF + here, 1), :] = delta


def grad_kernel(half, base, keep, aliased, slot_ref, pack_ref, kv_ref, stat_ref, *refs):
    refs = refs[aliased:]
    rows_ref = refs[0] if base == 0 else None
    dkv_ref = refs[1] if base == 0 else refs[0]
    (q_ref, do_ref, qt_ref, dot_ref, side_ref,
     lse_ref, delta_ref, dq_ref, out_ref, ds_ref, p_ref) = refs[-11:]
    here = pl.program_id(0)
    text = half * HALF + base + here

    @pl.when(here == 0)
    def _():
        set_up(slot_ref[0], qt_ref, side_ref)

    load_rows(slot_ref[1 + SLOTS + text], pack_ref, q_ref, do_ref, qt_ref, dot_ref)
    lses = [stat_ref[i, pl.ds(base + here, 1), :] for i in range(NZ)]
    top = lses[0]
    for i in range(1, NZ):
        top = jnp.maximum(top, lses[i])
    weights = [jnp.exp2((v - top) * SCALE2) for v in lses]
    total = weights[0]
    delta = weights[0] * stat_ref[0, pl.ds(HALF + base + here, 1), :]
    for i in range(1, NZ):
        total = total + weights[i]
        delta = delta + weights[i] * stat_ref[i, pl.ds(HALF + base + here, 1), :]
    lse = top + jnp.log2(total) * (1.0 / SCALE2)
    lse_ref[...] = lse
    delta_ref[...] = delta / total
    out_ref[...] = jnp.zeros(out_ref.shape, F32)
    dq_ref[...] = jnp.zeros(dq_ref.shape, F32)

    def slot(s):
        mark = slot_ref[1 + text * MAXT + s]
        owner = jnp.maximum(mark, 0)
        side = side_ref[jnp.where(mark < 0, SMP_DEV, owner)]
        k = slot_tokens(kv_ref, 0, s)
        v = slot_tokens(kv_ref, 1, s)
        sl = pl.ds(pl.multiple_of(owner * BL, BL), WIDE)
        sc = dot(jnp.concatenate([k, side], axis=1), qt_ref[:, sl], 1, 0)
        g = dot(v, dot_ref[:, sl], 1, 0)
        p = jnp.exp2((sc - lse_ref[:, sl]) * SCALE2)
        ds = (p * (g - delta_ref[:, sl])).astype(BF)
        p = p.astype(BF)
        if rows_ref is not None:
            out_ref[:, sl] += dot(v.T, p, 1, 0)
            dq_ref[:, sl] += dot(k.T, ds, 1, 0)
        if keep is None:
            tokens(s, sl, ds, p)
        else:
            ds_ref[s] = ds
            p_ref[s] = p

    def tokens(s, sl, ds, p):
        dk = dot(ds, q_ref[sl], 1, 0) * SCALE
        dv = dot(p, do_ref[sl], 1, 0)
        dkv_ref[:, 0, s] = dk.astype(BF).reshape(TOKS // 8, 8, HD)
        dkv_ref[:, 1, s] = dv.astype(BF).reshape(TOKS // 8, 8, HD)

    for s in range(MAXT):
        slot(s)
    if rows_ref is not None:
        rows_ref[0, 0] = out_ref[...].astype(BF)
        rows_ref[0, 1] = (dq_ref[...] * SCALE).astype(BF)
    if keep is not None:

        @pl.when(here < keep)
        def _():
            for s in range(MAXT):
                owner = jnp.maximum(slot_ref[1 + text * MAXT + s], 0)
                sl = pl.ds(pl.multiple_of(owner * BL, BL), WIDE)
                tokens(s, sl, ds_ref[s], p_ref[s])


def turn_kernel(rows_ref, out_ref, dq_ref):
    for j, ref in enumerate((out_ref, dq_ref)):
        for rb in range(RB):
            turned = rows_ref[0, j, :, rb * BL : (rb + 1) * BL].astype(F32).T.astype(BF)
            for h in range(HEADS):
                ref[rb * RBR : (rb + 1) * RBR, h * HD : (h + 1) * HD] = turned[
                    h * RBR : (h + 1) * RBR
                ]


def params(mib):
    return pltpu.CompilerParams(vmem_limit_bytes=mib * MIB)


def per_device(queries, keys, values, d_out, tile_sample, row_sample):
    z = lax.axis_index("z")
    c = lax.axis_index("c")
    tiles, patch, width = keys.shape
    plane = ("c", "tensor")

    mine = pl.pallas_call(
        pack_kernel,
        grid=(2,),
        in_specs=[pl.BlockSpec((ROWS, LANES), lambda i: (0, 0))] * 2,
        out_specs=pl.BlockSpec((ROWS, LANES), lambda i: (i, 0)),
        out_shape=jax.ShapeDtypeStruct((2 * ROWS, LANES), BF),
        compiler_params=params(56),
        name="pack",
    )(queries, d_out)
    pack = lax.all_gather(mine, "z", axis=0, tiled=False)

    mine_first = jnp.sum(jnp.where(row_sample == 0, 1.0, 0.0), axis=1, keepdims=True)
    mine_first = jnp.broadcast_to(mine_first, (1, HD))
    firsts = [mine_first] + [
        lax.ppermute(mine_first, "z", [(i, (i + by) % NZ) for i in range(NZ)])
        for by in range(1, NZ)
    ]
    back = (z - jnp.arange(NZ, dtype=jnp.int32) + NZ) % NZ
    firsts = jnp.concatenate(firsts, axis=0)[:, 0]
    firsts = jnp.sum(
        jnp.where(back[:, None] == jnp.arange(NZ, dtype=jnp.int32)[None, :], firsts[:, None], 0.0),
        axis=0,
    ).astype(jnp.int32)

    owner = tile_sample // SMP_DEV
    ids = jnp.arange(tiles, dtype=jnp.int32)
    rank = jnp.sum(
        ((owner[:, None] == owner[None, :]) & (ids[None, :] < ids[:, None])).astype(jnp.int32),
        axis=1, dtype=jnp.int32,
    )
    spot = (owner % NC) * SLOTS + (owner // NC) * MAXT + rank
    match = spot[None, :] == jnp.arange(NC * SLOTS, dtype=jnp.int32)[:, None]
    spot_tile = jnp.sum(jnp.where(match, ids[None, :] + 1, 0), axis=1, dtype=jnp.int32) - 1
    spot_sample = (
        jnp.sum(jnp.where(match, (tile_sample % SMP_DEV)[None, :] + 1, 0), axis=1, dtype=jnp.int32) - 1
    )
    slot_info = jnp.concatenate(
        [z.astype(jnp.int32)[None], lax.dynamic_slice_in_dim(spot_sample, c * SLOTS, SLOTS), firsts]
    )

    flat = lambda a: a.transpose(1, 0, 2).reshape(patch * tiles, width)
    depth = patch * tiles
    spots = NC * SLOTS
    pair = 2 * HD
    sent = pl.pallas_call(
        select_kernel,
        grid=(width // pair,),
        in_specs=[
            pl.BlockSpec((spots, 1), lambda i: (0, 0)),
            pl.BlockSpec((depth, pair), lambda i: (0, i)),
            pl.BlockSpec((depth, pair), lambda i: (0, i)),
        ],
        out_specs=pl.BlockSpec((NC, 2, 2, SLOTS * 8, HD), lambda i: (0, i, 0, 0, 0)),
        out_shape=jax.ShapeDtypeStruct((NC, KVH, 2, SLOTS * 8, HD), BF),
        scratch_shapes=[pltpu.VMEM((2, pair // HD, spots * 8, HD), F32)],
        compiler_params=params(56),
        name="select",
    )(spot_tile[:, None], flat(keys), flat(values))
    kv = lax.all_to_all(
        sent.reshape(NC * KVH, 2 * SLOTS * 8, HD), plane, 0, 0, tiled=True
    ).reshape(NC * KVH, 2, SLOTS, 8, HD)

    row_scratch = [
        pltpu.VMEM((LANES, HD), BF),
        pltpu.VMEM((LANES, HD), BF),
        pltpu.VMEM((2 * HD, LANES), BF),
        pltpu.VMEM((HD, LANES), BF),
        pltpu.VMEM((SMP_DEV + 1, TOKS, HD), BF),
        pltpu.VMEM((1, LANES), F32),
        pltpu.VMEM((1, LANES), F32),
    ]
    whole = pl.BlockSpec(memory_space=pltpu.VMEM)
    pack_specs = [
        pl.BlockSpec((1, 2 * ROWS, LANES), lambda i, *_, h=h: (h * HALF + i, 0, 0))
        for h in range(2)
    ]
    kv_specs = [
        pl.BlockSpec((NC * KVH, 2, MAXT, 8, HD), lambda i, *_, h=h: (0, 0, h * HALF + i, 0, 0))
        for h in range(2)
    ]
    parts = []
    for h in range(2):
        stat = pl.pallas_call(
            functools.partial(stats_kernel, h),
            grid_spec=pltpu.PrefetchScalarGridSpec(
                num_scalar_prefetch=1,
                grid=(HALF,),
                in_specs=[pack_specs[h], kv_specs[h]],
                out_specs=pl.BlockSpec((NZ, NZ, LANES), lambda i, *_: (0, 0, 0)),
                scratch_shapes=row_scratch + [pltpu.VMEM((1, LANES), F32)],
            ),
            out_shape=jax.ShapeDtypeStruct((NZ, NZ, LANES), F32),
            compiler_params=params(56),
            name=f"stats{h}",
        )(slot_info, pack, kv)
        parts.append(lax.all_to_all(stat, "z", 0, 0, tiled=True))

    rows_shape = jax.ShapeDtypeStruct((NZ, 2, HD, LANES), BF)
    dkv_shape = jax.ShapeDtypeStruct((NC * KVH, 2, SLOTS, 8, HD), BF)

    def grads(h, base, keep, made):
        first = h * HALF + base
        last = HALF - 1 if keep is None else keep - 1
        kv_block = (NC * KVH, 2, MAXT, 8, HD)
        rows_out = pl.BlockSpec((1, 2, HD, LANES), lambda i, *_: (first + i, 0, 0, 0))
        dkv_out = pl.BlockSpec(
            kv_block, lambda i, *_: (0, 0, first + jnp.minimum(i, last), 0, 0)
        )
        return pl.pallas_call(
            functools.partial(grad_kernel, h, base, keep, len(made)),
            grid_spec=pltpu.PrefetchScalarGridSpec(
                num_scalar_prefetch=1,
                grid=(HALF - base,),
                in_specs=[
                    pl.BlockSpec((1, 2 * ROWS, LANES), lambda i, *_: (first + i, 0, 0)),
                    pl.BlockSpec(kv_block, lambda i, *_: (0, 0, first + i, 0, 0)),
                    pl.BlockSpec((NZ, NZ, LANES), lambda i, *_: (0, 0, 0)),
                ]
                + [pl.BlockSpec(memory_space=pl.ANY)] * len(made),
                out_specs=[rows_out, dkv_out] if base == 0 else [dkv_out],
                scratch_shapes=row_scratch
                + [pltpu.VMEM((HD, LANES), F32)] * 2
                + [pltpu.VMEM((MAXT, TOKS, WIDE), BF)] * 2,
            ),
            out_shape=[rows_shape, dkv_shape] if base == 0 else [dkv_shape],
            input_output_aliases={4 + j: j for j in range(len(made))},
            compiler_params=params(56),
            name=f"grads{h}{base}",
        )(slot_info, pack, kv, parts[h], *made)

    made = grads(0, 0, None, ())
    rows, dkv = grads(1, 0, HALF // 2, made)
    (dkv,) = grads(1, HALF // 2, None, (dkv,))
    home = lax.psum_scatter(rows, "z", scatter_dimension=0, tiled=True)
    returned = lax.all_to_all(
        dkv.reshape(NC * KVH, 2 * SLOTS * 8, HD), plane, 0, 0, tiled=True
    ).reshape(NC, KVH, 2, SLOTS * 8, HD)

    d_key, d_value = pl.pallas_call(
        return_kernel,
        grid=(KVH,),
        in_specs=[
            pl.BlockSpec((tiles, 1), lambda i: (0, 0)),
            pl.BlockSpec((NC, 1, 2, SLOTS * 8, HD), lambda i: (0, i, 0, 0, 0)),
        ],
        out_specs=[pl.BlockSpec((depth, HD), lambda i: (0, i))] * 2,
        out_shape=[jax.ShapeDtypeStruct((depth, width), BF)] * 2,
        scratch_shapes=[pltpu.VMEM((2, spots * 8, HD), F32)],
        compiler_params=params(32),
        name="give_back",
    )(spot[:, None], returned)
    unflat = lambda a: a.reshape(patch, tiles, width).transpose(1, 0, 2)

    attn_out, d_query = pl.pallas_call(
        turn_kernel,
        out_shape=[jax.ShapeDtypeStruct((ROWS, LANES), BF)] * 2,
        compiler_params=params(56),
        name="turn",
    )(home)
    return (attn_out, d_query, unflat(d_key), unflat(d_value))


def solution(mesh):
    split = Mesh(mesh.devices.reshape(NZ, NC, KVH), ("z", "c", "tensor"))
    rows = P(("z", "c"), "tensor")
    tokens = P(None, ("z", "c", "tensor"), None)
    return jax.shard_map(
        per_device,
        mesh=split,
        in_specs=(rows, tokens, tokens, rows, P(), P(("z", "c"), None)),
        out_specs=(rows, rows, tokens, tokens),
        check_vma=False,
    )
```
